32 devices in a mesh: section: 4 (over y, x), band: 8 (over z, core).
Axes of the slice: x: 2, y: 2, z: 4, core: 2. Of those that a mesh axis runs over, the one named last changes fastest.
Arguments:
- control: bfloat16 [4, 512, 2, 128, 512], P('section', 'band'), may hold values from -6 to 6
- legendre: bfloat16 [512, 512, 512], P('band'), may hold values from -0.25 to 0.25
- spectral_sd: float32 [4, 512], P('section'), may hold values from 0.3 to 3
- vertical: bfloat16 [4, 128, 128], P('section'), may hold values from -0.5 to 0.5
- obs_lon: int32 [512, 1024], P('band'), may hold values from 0 to 1023
- obs_count: int32 [512], P('band'), may hold values from 1 to 1024, as said below
- kernels: bfloat16 [512, 1024, 128], P('band'), may hold values from 0 to 0.0039978027
- obs_value: float32 [512, 1024], P('band'), may hold values from -8 to 8
- obs_weight: float32 [512, 1024], P('band'), may hold values from 1 to 16
Outputs:
- gradient: bfloat16 [4, 512, 2, 128, 512], P('section', 'band')
- departures: float32 [512, 1024], P('band')
The draws below stay inside these ranges and needn't reach their ends.
Inputs may be any that keep to these rules, and one draw needn't show every extreme that they name: Slots 0 to obs_count - 1 of a latitude row hold its soundings, the others are empty; some row holds exactly 1024.
All inputs are finite; a program needn't handle non-finite values.
Results may differ from the reference program's by a relative error of at most 0.014.
Values may be sent and summed in bfloat16 or wider, within the bound.
A program may use at most 192 MiB of HBM per device.

```python
import math
import jax
import jax.numpy as jnp
from jax import lax

M = 512
N = 512
NLAT = 512
NLON = 1024
LEV = 128
KROW = 1024
COMPONENTS = 4


def draw_obs_count(key, part):
    base_key = jax.random.fold_in(key, 7)
    first_key, second_key, row_key = jax.random.split(base_key, 3)
    first_draw = jax.random.randint(first_key, (NLAT,), 0, KROW)
    second_draw = jax.random.randint(second_key, (NLAT,), 0, KROW)
    counts = KROW - first_draw * second_draw // (4 * KROW)
    chosen = jax.random.randint(row_key, (), 0, NLAT)
    return jnp.where(jnp.arange(NLAT) == chosen, KROW, counts).astype(jnp.int32)


def set_ends(result, key, low, high):
    extent = result.shape
    spot = [jax.random.randint(jax.random.fold_in(key, axis), (), 0, extent[axis]) for axis in range(len(extent))]
    result = result.at[tuple(spot)].set(low)
    longest = extent.index(max(extent))
    spot[longest] = (spot[longest] + 1) % extent[longest]
    return result.at[tuple(spot)].set(high)


def levels(key, shape, shards, least, top_value):
    def one(axis_at, blocks):
        heights = jax.random.uniform(jax.random.fold_in(jax.random.fold_in(key, 6), axis_at), (blocks,), jnp.float32, least / len(shards), top_value / len(shards))
        return jnp.repeat(jnp.exp(heights), shape[axis_at] // blocks).reshape((-1,) + (1,) * (len(shape) - axis_at - 1))

    gain = one(*shards[0])
    for cut in shards[1:]:
        gain = gain * one(*cut)
    return gain


def bell_draw(rng, shape, scale, limit, cuts=(), held_as=jnp.bfloat16):
    factor_of = levels(rng, shape, cuts, -0.22, 0.18) if cuts else 1.0
    result = jax.random.normal(rng, shape, jnp.float32) * scale * factor_of
    return jnp.minimum(jnp.maximum(result, -limit), limit).astype(held_as)


def setup_inputs(seed: int = 0) -> dict:
    arg_keys = jax.random.split(jax.random.key(seed), 10)
    return {
        "control": bell_draw(arg_keys[0], (COMPONENTS, M, 2, LEV, N), 1.0, 6.0, ((0, 4), (1, 8))),
        "legendre": bell_draw(arg_keys[1], (M, N, NLAT), N ** -0.5, 0.25, ((0, 8),)),
        "spectral_sd": jnp.clip(jnp.exp(math.log(3.0) - 2.3025851 * jax.random.uniform(arg_keys[2], (COMPONENTS, N), jnp.float32) ** levels(arg_keys[2], (COMPONENTS, N), ((0, 4),), -0.2, 0.2)), 0.3, 3.0),
        "vertical": bell_draw(arg_keys[3], (COMPONENTS, LEV, LEV), LEV ** -0.5, 0.5, ((0, 4),)),
        "obs_lon": set_ends(jax.random.randint(arg_keys[4], (NLAT, KROW), 0, NLON), jax.random.fold_in(arg_keys[4], 1), 0, NLON - 1).astype(jnp.int32),
        "obs_count": draw_obs_count(jax.random.fold_in(arg_keys[9], 71), 0),
        "kernels": jnp.clip(0.0039978027 * jax.random.uniform(arg_keys[6], (NLAT, KROW, LEV), jnp.float32) ** levels(arg_keys[6], (NLAT, KROW, LEV), ((0, 8),), -0.2, 0.2), 0.0, 0.0039978027).astype(jnp.bfloat16),
        "obs_value": bell_draw(arg_keys[7], (NLAT, KROW), 2.0, 8.0, ((0, 8),), jnp.float32),
        "obs_weight": jnp.clip(jnp.exp(math.log(16.0) - 2.7725887 * jax.random.uniform(arg_keys[8], (NLAT, KROW), jnp.float32) ** levels(arg_keys[8], (NLAT, KROW), ((0, 8),), -0.2, 0.2)), 1.0, 16.0),
    }


def make_basis(longitude):
    wave_ids = jnp.arange(M, dtype=jnp.int32)
    phase_idx = (longitude[..., None] * wave_ids) % NLON
    angles = phase_idx.astype(jnp.float32) * (2.0 * math.pi / NLON)
    wave_weight = jnp.where(wave_ids == 0, 1.0, 2.0).astype(jnp.float32)
    fourier = jnp.stack([wave_weight * jnp.cos(angles), -wave_weight * jnp.sin(angles)], axis=-2)
    return fourier.astype(jnp.bfloat16)


def reference(control, legendre, spectral_sd, vertical, obs_lon, obs_count, kernels, obs_value, obs_weight):
    legendre_wide = legendre.astype(jnp.float32)

    def add_component(field_sum, inputs):
        coeffs, spread, mixing = inputs
        scaled = (coeffs.astype(jnp.float32) * spread).astype(jnp.bfloat16)
        spectral_rows = jnp.einsum('mnj,mrkn->mjrk', legendre_wide, scaled.astype(jnp.float32)).astype(jnp.bfloat16)
        fields = jnp.einsum('mjrk,lk->mjrl', spectral_rows.astype(jnp.float32), mixing.astype(jnp.float32)).astype(jnp.bfloat16)
        return field_sum + fields.astype(jnp.float32), None

    start_sum = jnp.zeros((M, NLAT, 2, LEV), jnp.float32)
    field_sum, _ = lax.scan(add_component, start_sum, (control, spectral_sd, vertical))
    row_fields = jnp.moveaxis(field_sum, 1, 0)

    def row_evolve(inputs):
        longitude, field_row, kern_row = inputs
        fourier = make_basis(longitude).astype(jnp.float32)
        columns = jnp.einsum('qrm,mrl->ql', fourier, field_row, precision=lax.Precision.HIGHEST)
        return jnp.sum(kern_row.astype(jnp.float32) * columns, axis=-1)

    evolved = lax.map(row_evolve, (obs_lon, row_fields, kernels))
    slot_ids = lax.broadcasted_iota(jnp.int32, (NLAT, KROW), 1)
    is_live = slot_ids < obs_count[:, None]
    departures = jnp.where(is_live, evolved - obs_value, jnp.float32(0.0))
    adjoint_columns = ((obs_weight * departures)[:, :, None] * kernels.astype(jnp.float32)).astype(jnp.bfloat16)

    def row_adjoint(inputs):
        longitude, adjoint_row = inputs
        fourier = make_basis(longitude).astype(jnp.float32)
        return jnp.einsum('qrm,ql->mrl', fourier, adjoint_row.astype(jnp.float32)).astype(jnp.bfloat16)

    adjoint_stack = lax.map(row_adjoint, (obs_lon, adjoint_columns))
    adjoint_fields = jnp.moveaxis(adjoint_stack, 0, 1).astype(jnp.float32)

    def component_gradient(inputs):
        coeffs, spread, mixing = inputs
        adjoint_rows = jnp.einsum('mjrl,lk->mjrk', adjoint_fields, mixing.astype(jnp.float32)).astype(jnp.bfloat16)
        back_terms = jnp.einsum('mjrk,mnj->mrkn', adjoint_rows.astype(jnp.float32), legendre_wide)
        return (coeffs.astype(jnp.float32) + spread * back_terms).astype(jnp.bfloat16)

    gradient = lax.map(component_gradient, (control, spectral_sd, vertical))
    return gradient, departures
```

```python
import math

import jax
import jax.numpy as jnp
from jax import lax
from jax.sharding import PartitionSpec as P

NLON = 1024
CHUNKS = 4


def make_basis(longitude, wave_ids):
    waves = wave_ids.astype(jnp.float32)
    quarter = lax.broadcasted_iota(jnp.int32, (2, 1), 0).astype(jnp.float32) * 0.25
    turns = (longitude.astype(jnp.float32) * (1.0 / NLON))[..., None, None] * waves + quarter
    frac = turns - jnp.round(turns)
    x = 0.25 - jnp.abs(frac)
    z = x * x
    two_pi = 2.0 * math.pi
    coefs = [((-1) ** i) * two_pi ** (2 * i + 1) / math.factorial(2 * i + 1) for i in range(7)]
    acc = jnp.float32(coefs[-1])
    for coef in coefs[-2::-1]:
        acc = acc * z + jnp.float32(coef)
    weight = jnp.where(wave_ids == 0, 1.0, 2.0).astype(jnp.float32)
    return (acc * (x * weight)).astype(jnp.bfloat16)


def local(
    control, legendre, spectral_sd, vertical, obs_lon, obs_count, kernels, obs_value, obs_weight
):
    coeffs = control[0]
    spread = spectral_sd[0]
    mixing = vertical[0]
    local_rows = obs_lon.shape[0]
    wave_local, _, level_count, _ = coeffs.shape
    row_count = legendre.shape[2]
    section_count = lax.axis_size("section")
    band_count = lax.axis_size("band")
    row_share = local_rows // section_count
    first_row = lax.axis_index("section") * row_share
    chunks = math.gcd(CHUNKS, wave_local)
    step = wave_local // chunks

    own_lon = lax.dynamic_slice_in_dim(obs_lon, first_row, row_share, 0)
    own_count = lax.dynamic_slice_in_dim(obs_count, first_row, row_share, 0)
    own_kernels = lax.dynamic_slice_in_dim(kernels, first_row, row_share, 0)
    own_value = lax.dynamic_slice_in_dim(obs_value, first_row, row_share, 0)
    own_weight = lax.dynamic_slice_in_dim(obs_weight, first_row, row_share, 0)

    columns = 0.0
    bases = []
    for i in range(chunks):
        part = slice(i * step, (i + 1) * step)
        scaled = (coeffs[part].astype(jnp.float32) * spread).astype(jnp.bfloat16)
        spectral_rows = jnp.einsum(
            "mnj,mrkn->mjrk", legendre[part], scaled, preferred_element_type=jnp.float32
        ).astype(jnp.bfloat16)
        fields = jnp.einsum(
            "mjrk,lk->mjrl", spectral_rows, mixing, preferred_element_type=jnp.float32
        ).astype(jnp.bfloat16)
        stacked = fields.reshape(step, band_count, local_rows, 2, level_count)
        summed = lax.psum_scatter(stacked, "section", scatter_dimension=2, tiled=True)
        moved = lax.all_to_all(summed, "band", split_axis=1, concat_axis=0, tiled=True)[:, 0]
        wave_ids = (
            jnp.arange(band_count, dtype=jnp.int32)[:, None] * wave_local
            + i * step
            + jnp.arange(step, dtype=jnp.int32)
        ).reshape(-1)
        basis = make_basis(own_lon, wave_ids)
        bases.append(basis)
        columns = columns + jnp.einsum(
            "jqrm,mjrl->jql", basis, moved, preferred_element_type=jnp.float32
        )
    wide_kernels = own_kernels.astype(jnp.float32)
    evolved = jnp.sum(wide_kernels * columns, axis=2)
    slot_ids = lax.broadcasted_iota(jnp.int32, evolved.shape, 1)
    is_live = slot_ids < own_count[:, None]
    own_departures = jnp.where(is_live, evolved - own_value, jnp.float32(0.0))
    adjoint_columns = ((own_weight * own_departures)[:, :, None] * wide_kernels).astype(jnp.bfloat16)

    pieces = []
    for i in range(chunks):
        part = slice(i * step, (i + 1) * step)
        own_adjoint = jnp.einsum(
            "jqrm,jql->mjrl", bases[i], adjoint_columns, preferred_element_type=jnp.float32
        ).astype(jnp.bfloat16)
        returned = lax.all_to_all(
            own_adjoint[:, None], "band", split_axis=0, concat_axis=1, tiled=True
        )
        gathered = lax.all_gather(returned, "section", axis=2, tiled=True)
        adjoint_all = gathered.reshape(step, row_count, 2, level_count)
        back_rows = jnp.einsum(
            "mjrl,lk->mjrk", adjoint_all, mixing, preferred_element_type=jnp.float32
        ).astype(jnp.bfloat16)
        gradient_terms = jnp.einsum(
            "mjrk,mnj->mrkn", back_rows, legendre[part], preferred_element_type=jnp.float32
        )
        pieces.append(
            (coeffs[part].astype(jnp.float32) + spread * gradient_terms).astype(jnp.bfloat16)
        )
    departures = lax.all_gather(own_departures, "section", axis=0, tiled=True)
    return (jnp.concatenate(pieces, axis=0)[None], departures)


def solution(mesh):
    in_specs = (
        P("section", "band", None, None, None),
        P("band", None, None),
        P("section", None),
        P("section", None, None),
        P("band", None),
        P("band"),
        P("band", None, None),
        P("band", None),
        P("band", None),
    )
    out_specs = (P("section", "band", None, None, None), P("band", None))
    return jax.shard_map(local, mesh=mesh, in_specs=in_specs, out_specs=out_specs, check_vma=False)
```

```python
import math

import jax
import jax.numpy as jnp
from jax import lax
from jax.sharding import PartitionSpec as P

NLON = 1024
CHUNKS = 4


def make_basis(longitude, wave_ids):
    waves = wave_ids.astype(jnp.float32)
    quarter = lax.broadcasted_iota(jnp.int32, (2, 1), 0).astype(jnp.float32) * 0.25
    turns = (longitude.astype(jnp.float32) * (1.0 / NLON))[..., None, None] * waves + quarter
    frac = turns - jnp.round(turns)
    x = 0.25 - jnp.abs(frac)
    z = x * x
    two_pi = 2.0 * math.pi
    coefs = [((-1) ** i) * two_pi ** (2 * i + 1) / math.factorial(2 * i + 1) for i in range(7)]
    acc = jnp.float32(coefs[-1])
    for coef in coefs[-2::-1]:
        acc = acc * z + jnp.float32(coef)
    weight = jnp.where(wave_ids == 0, 1.0, 2.0).astype(jnp.float32)
    return (acc * (x * weight)).astype(jnp.bfloat16)


def exchange(block, bit):
    count = lax.axis_size("section")
    return lax.ppermute(block, "section", [(s, s ^ bit) for s in range(count)])


def side(bit):
    return (lax.axis_index("section") // bit) % 2


def pick(stacked, axis, index):
    return lax.dynamic_index_in_dim(stacked, index, axis, keepdims=False)


def add(kept, came):
    return (kept.astype(jnp.float32) + came.astype(jnp.float32)).astype(jnp.bfloat16)


def sum_rows(fields, band_count, first, second):
    step, row_count, parts, level_count = fields.shape
    section_count = lax.axis_size("section")
    if section_count != 4:
        stacked = fields.reshape(step, band_count, row_count // band_count, parts, level_count)
        return lax.psum_scatter(stacked, "section", scatter_dimension=2, tiled=True)
    block = fields.reshape(step, band_count, 2, 2, -1, parts, level_count)
    axis = 3 if first == 1 else 2
    came = exchange(pick(block, axis, 1 - side(first)), first)
    pair = add(pick(block, axis, side(first)), came)
    came = exchange(pick(pair, 2, 1 - side(second)), second)
    return add(pick(pair, 2, side(second)), came)


def gather_rows(returned, first, second):
    step, _, _, parts, level_count = returned.shape
    section_count = lax.axis_size("section")
    if section_count != 4:
        gathered = lax.all_gather(returned, "section", axis=2, tiled=True)
        return gathered.reshape(step, -1, parts, level_count), returned
    near = exchange(returned, first)
    far = exchange(returned, second)
    far_near = exchange(near, second)
    me = lax.axis_index("section")
    all_rows = jnp.zeros((4,) + returned.shape, returned.dtype)
    for block, flip in ((returned, 0), (near, first), (far, second), (far_near, first + second)):
        owner = me + flip - 2 * (me & flip)
        all_rows = lax.dynamic_update_index_in_dim(all_rows, block, owner, 0)
    ordered = jnp.transpose(all_rows, (1, 2, 0, 3, 4, 5))
    return ordered.reshape(step, -1, parts, level_count), near


def orders(index):
    return (1, 2) if index % 2 == 0 else (2, 1)


def local(
    control, legendre, spectral_sd, vertical, obs_lon, obs_count, kernels, obs_value, obs_weight
):
    coeffs = control[0]
    spread = spectral_sd[0]
    mixing = vertical[0]
    local_rows = obs_lon.shape[0]
    wave_local, _, level_count, _ = coeffs.shape
    row_count = legendre.shape[2]
    section_count = lax.axis_size("section")
    band_count = lax.axis_size("band")
    row_share = local_rows // section_count
    first_row = lax.axis_index("section") * row_share
    chunks = math.gcd(CHUNKS, wave_local)
    step = wave_local // chunks

    own_lon = lax.dynamic_slice_in_dim(obs_lon, first_row, row_share, 0)
    own_count = lax.dynamic_slice_in_dim(obs_count, first_row, row_share, 0)
    own_kernels = lax.dynamic_slice_in_dim(kernels, first_row, row_share, 0)
    own_value = lax.dynamic_slice_in_dim(obs_value, first_row, row_share, 0)
    own_weight = lax.dynamic_slice_in_dim(obs_weight, first_row, row_share, 0)

    columns = 0.0
    bases = []
    for i in range(chunks):
        part = slice(i * step, (i + 1) * step)
        halves = 2 if step % 2 == 0 else 1
        sums = []
        for h in range(halves):
            begin = i * step + h * (step // halves)
            sub = slice(begin, begin + step // halves)
            scaled = (coeffs[sub].astype(jnp.float32) * spread).astype(jnp.bfloat16)
            spectral_rows = jnp.einsum(
                "mnj,mrkn->mjrk", legendre[sub], scaled, preferred_element_type=jnp.float32
            ).astype(jnp.bfloat16)
            fields = jnp.einsum(
                "mjrk,lk->mjrl", spectral_rows, mixing, preferred_element_type=jnp.float32
            ).astype(jnp.bfloat16)
            sums.append(sum_rows(fields, band_count, *orders(h)))
        summed = jnp.concatenate(sums, axis=0)
        moved = lax.all_to_all(summed, "band", split_axis=1, concat_axis=0, tiled=True)[:, 0]
        wave_ids = (
            jnp.arange(band_count, dtype=jnp.int32)[:, None] * wave_local
            + i * step
            + jnp.arange(step, dtype=jnp.int32)
        ).reshape(-1)
        basis = make_basis(own_lon, wave_ids)
        bases.append(basis)
        columns = columns + jnp.einsum(
            "jqrm,mjrl->jql", basis, moved, preferred_element_type=jnp.float32
        )
    wide_kernels = own_kernels.astype(jnp.float32)
    evolved = jnp.sum(wide_kernels * columns, axis=2)
    slot_ids = lax.broadcasted_iota(jnp.int32, evolved.shape, 1)
    is_live = slot_ids < own_count[:, None]
    own_departures = jnp.where(is_live, evolved - own_value, jnp.float32(0.0))
    adjoint_columns = ((own_weight * own_departures)[:, :, None] * wide_kernels).astype(jnp.bfloat16)

    pieces = []
    nears = []
    for i in range(chunks):
        part = slice(i * step, (i + 1) * step)
        own_adjoint = jnp.einsum(
            "jqrm,jql->mjrl", bases[i], adjoint_columns, preferred_element_type=jnp.float32
        ).astype(jnp.bfloat16)
        by_band = own_adjoint.reshape(band_count, step, row_share, 2, level_count)
        outgoing = jnp.swapaxes(by_band, 0, 1)
        if i >= 2:
            outgoing, _ = lax.optimization_barrier((outgoing, nears[i - 2]))
        returned = lax.all_to_all(outgoing, "band", split_axis=1, concat_axis=1, tiled=True)
        adjoint_all, near = gather_rows(returned, *orders(i))
        nears.append(near)
        back_rows = jnp.einsum(
            "mjrl,lk->mjrk", adjoint_all, mixing, preferred_element_type=jnp.float32
        ).astype(jnp.bfloat16)
        gradient_terms = jnp.einsum(
            "mjrk,mnj->mrkn", back_rows, legendre[part], preferred_element_type=jnp.float32
        )
        pieces.append(
            (coeffs[part].astype(jnp.float32) + spread * gradient_terms).astype(jnp.bfloat16)
        )
    departures = lax.all_gather(own_departures, "section", axis=0, tiled=True)
    return (jnp.concatenate(pieces, axis=0)[None], departures)


def solution(mesh):
    in_specs = (
        P("section", "band", None, None, None),
        P("band", None, None),
        P("section", None),
        P("section", None, None),
        P("band", None),
        P("band"),
        P("band", None, None),
        P("band", None),
        P("band", None),
    )
    out_specs = (P("section", "band", None, None, None), P("band", None))
    return jax.shard_map(local, mesh=mesh, in_specs=in_specs, out_specs=out_specs, check_vma=False)
```

```python
import math

import jax
import jax.numpy as jnp
from jax import lax
from jax.sharding import PartitionSpec as P

NLON = 1024
CHUNKS = 4


def make_basis(longitude, wave_ids):
    waves = wave_ids.astype(jnp.float32)
    quarter = lax.broadcasted_iota(jnp.int32, (2, 1), 0).astype(jnp.float32) * 0.25
    turns = (longitude.astype(jnp.float32) * (1.0 / NLON))[..., None, None] * waves + quarter
    frac = turns - jnp.round(turns)
    x = 0.25 - jnp.abs(frac)
    z = x * x
    two_pi = 2.0 * math.pi
    coefs = [((-1) ** i) * two_pi ** (2 * i + 1) / math.factorial(2 * i + 1) for i in range(7)]
    acc = jnp.float32(coefs[-1])
    for coef in coefs[-2::-1]:
        acc = acc * z + jnp.float32(coef)
    weight = jnp.where(wave_ids == 0, 1.0, 2.0).astype(jnp.float32)
    return (acc * (x * weight)).astype(jnp.bfloat16)


def exchange(block, bit):
    count = lax.axis_size("section")
    return lax.ppermute(block, "section", [(s, s ^ bit) for s in range(count)])


def side(bit):
    return (lax.axis_index("section") // bit) % 2


def pick(stacked, axis, index):
    return lax.dynamic_index_in_dim(stacked, index, axis, keepdims=False)


def add(kept, came):
    return (kept.astype(jnp.float32) + came.astype(jnp.float32)).astype(jnp.bfloat16)


def sum_rows(fields, band_count, first, second):
    step, row_count, parts, level_count = fields.shape
    section_count = lax.axis_size("section")
    if section_count != 4:
        stacked = fields.reshape(step, band_count, row_count // band_count, parts, level_count)
        return lax.psum_scatter(stacked, "section", scatter_dimension=2, tiled=True)
    block = fields.reshape(step, band_count, 2, 2, -1, parts, level_count)
    axis = 3 if first == 1 else 2
    came = exchange(pick(block, axis, 1 - side(first)), first)
    pair = add(pick(block, axis, side(first)), came)
    came = exchange(pick(pair, 2, 1 - side(second)), second)
    return add(pick(pair, 2, side(second)), came)


def gather_rows(returned, first, second):
    step, _, _, parts, level_count = returned.shape
    section_count = lax.axis_size("section")
    if section_count != 4:
        gathered = lax.all_gather(returned, "section", axis=2, tiled=True)
        return gathered.reshape(step, -1, parts, level_count), returned
    near = exchange(returned, first)
    far = exchange(returned, second)
    far_near = exchange(near, second)
    me = lax.axis_index("section")
    all_rows = jnp.zeros((4,) + returned.shape, returned.dtype)
    for block, flip in ((returned, 0), (near, first), (far, second), (far_near, first + second)):
        owner = me + flip - 2 * (me & flip)
        all_rows = lax.dynamic_update_index_in_dim(all_rows, block, owner, 0)
    ordered = jnp.transpose(all_rows, (1, 2, 0, 3, 4, 5))
    return ordered.reshape(step, -1, parts, level_count), near


def orders(index):
    return (1, 2) if index % 2 == 0 else (2, 1)


def local(
    control, legendre, spectral_sd, vertical, obs_lon, obs_count, kernels, obs_value, obs_weight
):
    coeffs = control[0]
    spread = spectral_sd[0]
    mixing = vertical[0]
    local_rows = obs_lon.shape[0]
    wave_local, _, level_count, _ = coeffs.shape
    row_count = legendre.shape[2]
    section_count = lax.axis_size("section")
    band_count = lax.axis_size("band")
    row_share = local_rows // section_count
    first_row = lax.axis_index("section") * row_share
    chunks = math.gcd(CHUNKS, wave_local)
    step = wave_local // chunks

    own_lon = lax.dynamic_slice_in_dim(obs_lon, first_row, row_share, 0)
    own_count = lax.dynamic_slice_in_dim(obs_count, first_row, row_share, 0)
    own_kernels = lax.dynamic_slice_in_dim(kernels, first_row, row_share, 0)
    own_value = lax.dynamic_slice_in_dim(obs_value, first_row, row_share, 0)
    own_weight = lax.dynamic_slice_in_dim(obs_weight, first_row, row_share, 0)

    columns = 0.0
    bases = []
    for i in range(chunks):
        part = slice(i * step, (i + 1) * step)
        halves = 2 if step % 2 == 0 else 1
        sums = []
        for h in range(halves):
            begin = i * step + h * (step // halves)
            sub = slice(begin, begin + step // halves)
            scaled = (coeffs[sub].astype(jnp.float32) * spread).astype(jnp.bfloat16)
            spectral_rows = jnp.einsum(
                "mnj,mrkn->mjrk", legendre[sub], scaled, preferred_element_type=jnp.float32
            ).astype(jnp.bfloat16)
            fields = jnp.einsum(
                "mjrk,lk->mjrl", spectral_rows, mixing, preferred_element_type=jnp.float32
            ).astype(jnp.bfloat16)
            sums.append(sum_rows(fields, band_count, *orders(h)))
        summed = jnp.concatenate(sums, axis=0)
        moved = lax.all_to_all(summed, "band", split_axis=1, concat_axis=0, tiled=True)[:, 0]
        wave_ids = (
            jnp.arange(band_count, dtype=jnp.int32)[:, None] * wave_local
            + i * step
            + jnp.arange(step, dtype=jnp.int32)
        ).reshape(-1)
        chunk_lon, moved = lax.optimization_barrier((own_lon, moved))
        basis = make_basis(chunk_lon, wave_ids)
        bases.append(basis)
        columns = columns + jnp.einsum(
            "jqrm,mjrl->jql", basis, moved, preferred_element_type=jnp.float32
        )
    wide_kernels = own_kernels.astype(jnp.float32)
    evolved = jnp.sum(wide_kernels * columns, axis=2)
    slot_ids = lax.broadcasted_iota(jnp.int32, evolved.shape, 1)
    is_live = slot_ids < own_count[:, None]
    own_departures = jnp.where(is_live, evolved - own_value, jnp.float32(0.0))
    adjoint_columns = ((own_weight * own_departures)[:, :, None] * wide_kernels).astype(jnp.bfloat16)

    pieces = []
    nears = []
    for i in range(chunks):
        part = slice(i * step, (i + 1) * step)
        own_adjoint = jnp.einsum(
            "jqrm,jql->mjrl", bases[i], adjoint_columns, preferred_element_type=jnp.float32
        ).astype(jnp.bfloat16)
        by_band = own_adjoint.reshape(band_count, step, row_share, 2, level_count)
        outgoing = jnp.swapaxes(by_band, 0, 1)
        if i >= 2:
            outgoing, _ = lax.optimization_barrier((outgoing, nears[i - 2]))
        returned = lax.all_to_all(outgoing, "band", split_axis=1, concat_axis=1, tiled=True)
        adjoint_all, near = gather_rows(returned, *orders(i))
        nears.append(near)
        back_rows = jnp.einsum(
            "mjrl,lk->mjrk", adjoint_all, mixing, preferred_element_type=jnp.float32
        ).astype(jnp.bfloat16)
        gradient_terms = jnp.einsum(
            "mjrk,mnj->mrkn", back_rows, legendre[part], preferred_element_type=jnp.float32
        )
        pieces.append(
            (coeffs[part].astype(jnp.float32) + spread * gradient_terms).astype(jnp.bfloat16)
        )
    departures = lax.all_gather(own_departures, "section", axis=0, tiled=True)
    return (jnp.concatenate(pieces, axis=0)[None], departures)


def solution(mesh):
    in_specs = (
        P("section", "band", None, None, None),
        P("band", None, None),
        P("section", None),
        P("section", None, None),
        P("band", None),
        P("band"),
        P("band", None, None),
        P("band", None),
        P("band", None),
    )
    out_specs = (P("section", "band", None, None, None), P("band", None))
    return jax.shard_map(local, mesh=mesh, in_specs=in_specs, out_specs=out_specs, check_vma=False)
```
